512 devices in a mesh: dp: 8 (over x, core), expert: 64 (over z, y).
Axes of the slice: x: 4, y: 4, z: 16, core: 2. Of those that a mesh axis runs over, the one named last changes fastest.
Arguments:
- tokens: bfloat16 [2560, 3584], P('expert', 'dp'), may hold values from -6 to 6
- cotangent: bfloat16 [2560, 3584], P('expert', 'dp'), may hold values from -1.1953125 to 1.1953125
- expert_ids: int32 [2560, 8], P('expert'), may hold values from 0 to 31, all different within a row; in each aligned block of 40 rows (0 to 39, 40 to 79, ...) at most 20 rows name the same one
- route_weight: bfloat16 [2560, 8], P('expert'), may hold values from 0.099609375 to 1
- gate_weight: bfloat16 [64, 3584, 512], P('expert', 'dp'), may hold values from -0.09375 to 0.09375
- up_weight: bfloat16 [64, 3584, 512], P('expert', 'dp'), may hold values from -0.09375 to 0.09375
- down_weight: bfloat16 [64, 512, 3584], P('expert', None, 'dp'), may hold values from -0.1875 to 0.1875
Outputs:
- token_grad: bfloat16 [2560, 3584], P('expert', 'dp')
- route_grad: bfloat16 [2560, 8], P('expert')
- gate_grad: bfloat16 [64, 3584, 512], P('expert', 'dp')
- up_grad: bfloat16 [64, 3584, 512], P('expert', 'dp')
- down_grad: bfloat16 [64, 512, 3584], P('expert', None, 'dp')
The draws below stay inside these ranges and needn't reach their ends.
Inputs may be any that keep to these rules, and one draw needn't show every extreme that they name: `expert_ids`: each row names distinct experts. In each aligned block of 40 rows no expert is named by more than 20 rows, a bound that some block reaches.
All inputs are finite; a program needn't handle non-finite values.
Results may differ from the reference program's by a relative error of at most 0.034.
Values may be sent and summed in bfloat16 or wider, within the bound.
No kernel may reach another device: no remote copies, remote signals or barrier semaphores. Data moves between devices by JAX's collectives and lax.ppermute only.
A program may use at most 64 MiB of HBM per device.

```python
import math
import jax
import jax.numpy as jnp
import numpy as np
from jax import lax

D = 3584
HID = 1024
TOPK = 8
TOK_DEV = 40
EXPERTS = 32
CAPACITY = 20
TOKENS = 2560
N_DP = 8
N_EXPERT = 64


def level_of(key, shape, shards, low, high):
    level, own = 1.0, jax.random.fold_in(key, 6)
    for axis_at, shards_of in shards:
        heights = jnp.exp(jax.random.uniform(jax.random.fold_in(own, axis_at), (shards_of,), jnp.float32, low / len(shards), high / len(shards)))
        level = level * jnp.repeat(heights, shape[axis_at] // shards_of).reshape([-1 if axis == axis_at else 1 for axis in range(len(shape))])
    return level


def shared_out(rng, own, number, rows, amount, top, most, slope):
    ranking = jax.random.permutation(rng, amount)
    crowded, usual = load_shares(amount, rows * top, most, slope, True), load_shares(amount, rows * top, most, slope, False)
    places = jnp.arange(amount)

    def named(sizes, rotation):
        used = int((sizes > 0).sum())
        fixed = max(1, used // 4)
        shifted = fixed + (places - fixed + rotation * (used - fixed)) % max(1, amount - fixed)
        return jnp.zeros((amount,), jnp.int32).at[ranking[jnp.where(places < fixed, places, shifted)]].set(jnp.asarray(sizes, jnp.int32))

    sizes = jnp.where(number % 4 == 0, named(crowded, number // 4), named(usual, number - number // 4 - 1))
    mixed = jax.random.permutation(jax.random.fold_in(own, 3), amount)
    donor, taker = mixed[0:amount // 2 * 2:2], mixed[1:amount // 2 * 2:2]
    margin = jnp.minimum(sizes[donor] - 1, most - sizes[taker]) // 2
    margin = jnp.where((donor == ranking[0]) | (taker == ranking[0]) | (sizes[taker] == 0), 0, jnp.maximum(margin, 0))
    shifted = jax.random.randint(jax.random.fold_in(own, 4), (amount // 2,), 0, 1 << 20) % (margin + 1)
    sizes = sizes.at[donor].add(-shifted).at[taker].add(shifted)
    items = jnp.searchsorted(jnp.cumsum(sizes), jnp.arange(rows * top), side="right").astype(jnp.int32)
    grid = items.reshape(top, rows).T
    grid = grid[jax.random.permutation(jax.random.fold_in(own, 1), rows)]
    rotation = jax.random.randint(jax.random.fold_in(own, 2), (rows, 1), 0, top)
    return jnp.take_along_axis(grid, (jnp.arange(top)[None, :] + rotation) % top, axis=1)


def load_shares(count, total, most, slope, full):
    portions = [(1 << 20) // math.isqrt(grade ** slope) + 1 for grade in range(1, count + 1)]
    largest = most if full else min(most, max(-(-total // count), total * portions[0] // sum(portions)))
    least = 1 if total - largest >= count - 1 else 0
    holding, spare = [largest] + [least] * (count - 1), total - largest - least * (count - 1)
    while spare > 0:
        candidates = [i for i in range(1, count) if holding[i] < largest] or [i for i in range(1, count) if holding[i] < most]
        mass, budget = sum([portions[i] for i in candidates]), spare
        for i in candidates:
            extra = min(most - holding[i], max(1, budget * portions[i] // mass), spare)
            holding[i] = holding[i] + extra
            spare = spare - extra
    return np.array(holding)


def gaussian(stream_key, shape, deviation, most, shards=(), held_as=jnp.bfloat16):
    factor_of = level_of(stream_key, shape, shards, -0.22, 0.18) if shards else 1.0
    values = jax.random.normal(stream_key, shape, jnp.float32) * deviation * factor_of
    return jnp.minimum(jnp.maximum(values, -most), most).astype(held_as)


def setup_inputs(seed: int = 0) -> dict:
    key_of = jax.random.split(jax.random.key(seed), 8)
    tokens = gaussian(key_of[0], (TOKENS, D), 1.0, 6.0, ((0, 64), (1, 8)))
    cotangent = gaussian(key_of[1], (TOKENS, D), 0.2, 1.1953125, ((0, 64), (1, 8)))
    expert_ids_keys = jax.random.split(jax.random.fold_in(key_of[2], 1), TOKENS // TOK_DEV)
    expert_ids_turns = jax.random.permutation(jax.random.fold_in(key_of[2], 3), TOKENS // TOK_DEV)
    expert_ids = jax.vmap(lambda own, number: shared_out(jax.random.fold_in(key_of[2], 2), own, number, TOK_DEV, EXPERTS, TOPK, CAPACITY, 2))(expert_ids_keys, expert_ids_turns).reshape((TOKENS, TOPK))
    route_weight = jnp.clip(jnp.exp(math.log(1.0) - 2.306499 * jax.random.uniform(key_of[3], (TOKENS, TOPK), jnp.float32) ** level_of(key_of[3], (TOKENS, TOPK), ((0, 64),), -0.2, 0.2)), 0.099609375, 1.0).astype(jnp.bfloat16)
    gate_weight = gaussian(key_of[4], (N_EXPERT, D, HID // 2), D ** -0.5, 0.09375, ((0, 64), (1, 8)))
    up_weight = gaussian(key_of[5], (N_EXPERT, D, HID // 2), D ** -0.5, 0.09375, ((0, 64), (1, 8)))
    down_weight = gaussian(key_of[6], (N_EXPERT, HID // 2, D), HID ** -0.5, 0.1875, ((0, 64), (2, 8)))
    return dict(tokens=tokens, cotangent=cotangent, expert_ids=expert_ids, route_weight=route_weight, gate_weight=gate_weight, up_weight=up_weight, down_weight=down_weight)


def block_sum(values, weights):
    pieces = jnp.einsum("tqb,qbh->qth", values, weights)
    pieces = lax.optimization_barrier(pieces.astype(jnp.bfloat16))
    return jnp.sum(pieces.astype(jnp.float32), axis=0)


def activate(gate_pre, up_pre, hidden_grad, scale):
    sigmoid_g = jax.nn.sigmoid(gate_pre)
    hidden = (gate_pre * sigmoid_g * up_pre).astype(jnp.bfloat16)
    hidden_f = hidden.astype(jnp.float32)
    slot_dots = jnp.sum(hidden_f * hidden_grad, axis=1)
    scaled = (scale * hidden_f).astype(jnp.bfloat16)
    act_grad = scale * hidden_grad
    gate_g = (act_grad * up_pre * sigmoid_g * (1.0 + gate_pre * (1.0 - sigmoid_g))).astype(jnp.bfloat16)
    up_g = (act_grad * gate_pre * sigmoid_g).astype(jnp.bfloat16)
    return scaled, gate_g, up_g, slot_dots


def reference(tokens, cotangent, expert_ids, route_weight, gate_weight, up_weight, down_weight):
    half_hid = HID // 2
    block = D // N_DP
    limit = N_EXPERT * CAPACITY
    gate_all = jnp.transpose(gate_weight.reshape(EXPERTS, 2, D, half_hid), (0, 2, 1, 3)).reshape(EXPERTS, D, HID)
    up_all = jnp.transpose(up_weight.reshape(EXPERTS, 2, D, half_hid), (0, 2, 1, 3)).reshape(EXPERTS, D, HID)
    down_all = down_weight.reshape(EXPERTS, HID, D)
    weight_f = route_weight.astype(jnp.float32)

    def one_expert(running, inputs):
        expert, gate_mat, up_mat, down_mat = inputs
        grad_acc, route_acc = running
        named = expert_ids == expert
        scale_tok = jnp.sum(jnp.where(named, weight_f, 0.0), axis=1)
        present = jnp.any(named, axis=1)
        picked = jnp.nonzero(present, size=limit, fill_value=0)[0].astype(jnp.int32)
        is_live = jnp.arange(limit, dtype=jnp.int32) < jnp.sum(present.astype(jnp.int32))
        scale = jnp.where(is_live, scale_tok[picked], 0.0)[:, None]
        exp_tokens = tokens[picked]
        exp_cotan = cotangent[picked]
        grouped_x = exp_tokens.astype(jnp.float32).reshape(limit, N_DP, block)
        grouped_dy = exp_cotan.astype(jnp.float32).reshape(limit, N_DP, block)
        gate_pre = block_sum(grouped_x, gate_mat.astype(jnp.float32).reshape(N_DP, block, HID))
        up_pre = block_sum(grouped_x, up_mat.astype(jnp.float32).reshape(N_DP, block, HID))
        hidden_grad = block_sum(grouped_dy, jnp.transpose(down_mat).astype(jnp.float32).reshape(N_DP, block, HID))
        scaled, gate_g, up_g, slot_dots = activate(gate_pre, up_pre, hidden_grad, scale)
        down_g = jnp.dot(scaled.T, exp_cotan, preferred_element_type=jnp.float32).astype(jnp.bfloat16)
        gate_w = jnp.dot(exp_tokens.T, gate_g, preferred_element_type=jnp.float32).astype(jnp.bfloat16)
        up_w = jnp.dot(exp_tokens.T, up_g, preferred_element_type=jnp.float32).astype(jnp.bfloat16)
        token_back = jnp.dot(gate_g, gate_mat.T, preferred_element_type=jnp.float32)
        token_back = token_back + jnp.dot(up_g, up_mat.T, preferred_element_type=jnp.float32)
        token_back = lax.optimization_barrier(token_back.astype(jnp.bfloat16)).astype(jnp.float32)
        token_back = jnp.where(is_live[:, None], token_back, 0.0)
        dots_round = lax.optimization_barrier(slot_dots.astype(jnp.bfloat16)).astype(jnp.float32)
        dots_round = jnp.where(is_live, dots_round, 0.0)
        grad_acc = grad_acc.at[picked].add(token_back)
        per_token = jnp.zeros((TOKENS,), jnp.float32).at[picked].add(dots_round)
        route_acc = route_acc + jnp.where(named, per_token[:, None], 0.0)
        return (grad_acc, route_acc), (gate_w, up_w, down_g)

    start = (jnp.zeros((TOKENS, D), jnp.float32), jnp.zeros((TOKENS, TOPK), jnp.float32))
    series = (jnp.arange(EXPERTS, dtype=jnp.int32), gate_all, up_all, down_all)
    (grad_acc, route_acc), (gate_w, up_w, down_g) = lax.scan(one_expert, start, series)
    gate_out = jnp.transpose(gate_w.reshape(EXPERTS, D, 2, half_hid), (0, 2, 1, 3)).reshape(N_EXPERT, D, half_hid)
    up_out = jnp.transpose(up_w.reshape(EXPERTS, D, 2, half_hid), (0, 2, 1, 3)).reshape(N_EXPERT, D, half_hid)
    down_out = down_g.reshape(N_EXPERT, half_hid, D)
    return (grad_acc.astype(jnp.bfloat16), route_acc.astype(jnp.bfloat16), gate_out, up_out, down_out)
```

```python
import jax
import jax.numpy as jnp
from jax import lax
from jax.sharding import Mesh, PartitionSpec as P

BF = jnp.bfloat16
F32 = jnp.float32
FEAT = 448
WIDE = 512
CAP = 20


def dot(a, b, dims):
    return lax.dot_general(a, b, (dims, ((), ())), preferred_element_type=F32)


def take(a, axis, step):
    n = lax.axis_size(axis)
    return lax.ppermute(a, axis, [((i + step) % n, i) for i in range(n)])


def gather_z(a):
    rows = a.shape[0]
    far = jnp.concatenate([take(a, "z", 4), a, take(a, "z", -4), take(a, "z", 8)], 0)
    return jnp.concatenate(
        [
            far,
            take(far, "z", 1),
            take(far, "z", -1),
            take(far[: 2 * rows], "z", 2),
            take(far[rows : 3 * rows], "z", -2),
        ],
        0,
    )


def reduce_z(d, rows):
    f = lambda a: a.astype(F32)
    one = take(d[4 * rows : 8 * rows], "z", -1)
    back_one = take(d[8 * rows : 12 * rows], "z", 1)
    two = take(d[12 * rows : 14 * rows], "z", -2)
    back_two = take(d[14 * rows : 16 * rows], "z", 2)
    zero = jnp.zeros((rows, d.shape[1]), F32)
    s = f(d[: 4 * rows]) + f(one) + f(back_one)
    s = s + jnp.concatenate([f(two), zero, zero], 0)
    s = s + jnp.concatenate([zero, f(back_two), zero], 0)
    s = s.astype(BF)
    return (
        f(s[rows : 2 * rows])
        + f(take(s[:rows], "z", -4))
        + f(take(s[2 * rows : 3 * rows], "z", 4))
        + f(take(s[3 * rows :], "z", 8))
    )


def swap_core(a):
    return lax.ppermute(a, "core", [(0, 1), (1, 0)])


def trade(a, axis):
    return lax.all_to_all(a, axis, split_axis=0, concat_axis=0, tiled=True)


def on_device(tokens, cotangent, expert_ids, route_weight, gate_weight, up_weight, down_weight):
    rows = tokens.shape[0]
    core = lax.axis_index("core")
    xpos = lax.axis_index("x")
    z = lax.axis_index("z")
    experts = 32
    match = (expert_ids[:, :, None] == jnp.arange(experts, dtype=jnp.int32)).astype(F32)
    named = jnp.sum(match, axis=1)
    below = (jnp.arange(rows)[:, None] > jnp.arange(rows)[None, :]).astype(F32)
    rank = jnp.sum(match * dot(below, named, ((1,), (0,)))[:, None, :], axis=2)
    payload_x = jnp.concatenate(
        [tokens, expert_ids.astype(BF), rank.astype(BF), route_weight, jnp.zeros((rows, 40), BF)], 1
    )
    all_x = gather_z(payload_x)
    all_dy = gather_z(cotangent)
    total = all_x.shape[0]
    ids = all_x[:, FEAT : FEAT + 8]
    ranks = all_x[:, FEAT + 8 : FEAT + 16].astype(F32)
    weights = all_x[:, FEAT + 16 : FEAT + 24].astype(F32)
    half_rows = total // 2 // 2
    blocks = jnp.arange(total, dtype=jnp.int32) // rows

    def choose(which):
        hit = ids == (2 * z + which).astype(BF)
        live = jnp.any(hit, axis=1)
        place = jnp.sum(jnp.where(hit, ranks, 0.0), axis=1).astype(jnp.int32)
        place = (blocks * CAP + place + core * half_rows) % (2 * half_rows)
        place = jnp.where(live, place, -1)
        scale = jnp.sum(jnp.where(hit, weights, 0.0), axis=1)
        one_hot = (place[:, None] == jnp.arange(2 * half_rows, dtype=jnp.int32)).astype(BF)
        return hit, one_hot, scale.astype(BF)

    hit_a, pick_a, scale_a = choose(0)
    hit_b, pick_b, scale_b = choose(1)
    with_a = jnp.concatenate([all_x[:, :FEAT], scale_a[:, None], jnp.zeros((total, 63), BF)], 1)
    with_b = jnp.concatenate([all_x[:, :FEAT], scale_b[:, None], jnp.zeros((total, 63), BF)], 1)
    rows_dim = ((0,), (0,))
    x_a = dot(pick_a, with_a, rows_dim).astype(BF)
    x_b = dot(pick_b, with_b, rows_dim).astype(BF)
    got_x = trade(jnp.stack([x_a, x_a, x_b, x_b]), "y")
    dy_a = dot(pick_a, all_dy, rows_dim).astype(BF)
    dy_b = dot(pick_b, all_dy, rows_dim).astype(BF)
    got_dy = trade(jnp.stack([dy_a, dy_a, dy_b, dy_b]), "y")
    half = 4 * half_rows
    own_x = got_x[:, :half_rows].reshape(half, WIDE)
    oth_x = got_x[:, half_rows:].reshape(half, WIDE)
    own_dy = got_dy[:, :half_rows].reshape(half, FEAT)
    oth_dy = got_dy[:, half_rows:].reshape(half, FEAT)
    gate_mat, up_mat, down_mat = gate_weight[0], up_weight[0], down_weight[0]
    last_first = ((1,), (0,))
    last_last = ((1,), (1,))

    def reduce_dp(mine, others):
        pair = (mine + swap_core(others.astype(BF)).astype(F32)).astype(BF)
        pieces = trade(pair.reshape(4, half // 4, pair.shape[1]), "x")
        return jnp.sum(pieces.astype(F32), axis=0)

    gate_up = jnp.concatenate([gate_mat, up_mat], 1)
    gu = reduce_dp(
        dot(own_x[:, :FEAT], gate_up, last_first), dot(oth_x[:, :FEAT], gate_up, last_first)
    )
    hidden_grad = reduce_dp(
        dot(own_dy, down_mat, last_last), dot(oth_dy, down_mat, last_last)
    )
    hid = gate_mat.shape[1]
    gate_pre, up_pre = gu[:, :hid], gu[:, hid:]
    quarter = half // 4
    scale = lax.dynamic_slice_in_dim(own_x[:, FEAT : FEAT + 1], xpos * quarter, quarter, 0).astype(
        F32
    )
    sig = jax.nn.sigmoid(gate_pre)
    hidden = (gate_pre * sig * up_pre).astype(BF)
    hidden_f = hidden.astype(F32)
    dots = jnp.sum(hidden_f * hidden_grad, axis=1, keepdims=True).astype(BF)
    scaled = (scale * hidden_f).astype(BF)
    act_grad = scale * hidden_grad
    gate_g = (act_grad * up_pre * sig * (1.0 + gate_pre * (1.0 - sig))).astype(BF)
    up_g = (act_grad * gate_pre * sig).astype(BF)

    def spread_dp(a):
        mine = trade(jnp.broadcast_to(a[None], (4,) + a.shape), "x").reshape(half, a.shape[1])
        return mine, swap_core(mine)

    own_g, oth_g = spread_dp(
        jnp.concatenate([gate_g, up_g, jnp.pad(dots, ((0, 0), (0, 127)))], 1)
    )
    own_s, oth_s = spread_dp(scaled)

    def back(g):
        t = dot(g[:, :hid], gate_mat, last_last) + dot(g[:, hid : 2 * hid], up_mat, last_last)
        t = jnp.concatenate([t.astype(BF), g[:, 2 * hid : 2 * hid + 64]], 1)
        return t.reshape(4, half_rows, WIDE)

    ret = trade(jnp.concatenate([back(own_g), back(oth_g)], 1), "y").astype(F32)
    slot_a = (ret[0] + ret[1]).astype(BF)
    slot_b = (ret[2] + ret[3]).astype(BF)
    sum_a = dot(pick_a, slot_a, last_first)
    sum_b = dot(pick_b, slot_b, last_first)
    route = jnp.where(hit_a, sum_a[:, FEAT : FEAT + 1], 0.0) + jnp.where(
        hit_b, sum_b[:, FEAT : FEAT + 1], 0.0
    )
    dense = jnp.concatenate(
        [(sum_a + sum_b)[:, :FEAT].astype(BF), route.astype(BF), jnp.zeros((total, 56), BF)], 1
    )
    final = reduce_z(dense, rows).astype(BF)

    def wgrad(own_l, oth_l, own_r, oth_r):
        return (dot(own_l, own_r, rows_dim) + dot(oth_l, oth_r, rows_dim)).astype(BF)

    down_g = wgrad(own_s, oth_s, own_dy, oth_dy)
    gate_w = wgrad(own_x[:, :FEAT], oth_x[:, :FEAT], own_g[:, :hid], oth_g[:, :hid])
    up_w = wgrad(
        own_x[:, :FEAT], oth_x[:, :FEAT], own_g[:, hid : 2 * hid], oth_g[:, hid : 2 * hid]
    )
    return (final[:, :FEAT], final[:, FEAT : FEAT + 8], gate_w[None], up_w[None], down_g[None])


def solution(mesh):
    fine = Mesh(mesh.devices.reshape(4, 2, 16, 4), ("x", "core", "z", "y"))
    dp, expert = ("x", "core"), ("z", "y")
    return jax.shard_map(
        on_device,
        mesh=fine,
        in_specs=(
            P(expert, dp),
            P(expert, dp),
            P(expert, None),
            P(expert, None),
            P(expert, dp, None),
            P(expert, dp, None),
            P(expert, None, dp),
        ),
        out_specs=(
            P(expert, dp),
            P(expert, None),
            P(expert, dp, None),
            P(expert, dp, None),
            P(expert, None, dp),
        ),
        check_vma=False,
    )
```

```python
import jax
import jax.numpy as jnp
from jax import lax
from jax.experimental import pallas as pl
from jax.experimental.pallas import tpu as pltpu
from jax.sharding import Mesh, PartitionSpec as P

BF = jnp.bfloat16
F32 = jnp.float32
I32 = jnp.int32
TOK = 40
FEAT = 448
WIDE = 512
HALF = 512
CAP = 20
ALL = 640
PART = 160
ROWS = 320
EXP = 32


def dot(a, b, dims=((1,), (0,))):
    return lax.dot_general(a, b, (dims, ((), ())), preferred_element_type=F32)


LAST = ((1,), (1,))
FIRST = ((0,), (0,))


def call(body, outs, *args, scratch=(), flops=0):
    moved = sum(a.size * a.dtype.itemsize for a in args[1:])
    specs = [pl.BlockSpec(memory_space=pltpu.SMEM)]
    specs += [pl.BlockSpec(memory_space=pltpu.VMEM)] * (len(args) - 1)
    return pl.pallas_call(
        body,
        out_shape=[jax.ShapeDtypeStruct(s, d) for s, d in outs],
        in_specs=specs,
        out_specs=[pl.BlockSpec(memory_space=pltpu.VMEM)] * len(outs),
        scratch_shapes=list(scratch),
        compiler_params=pltpu.CompilerParams(vmem_limit_bytes=24 << 20),
        cost_estimate=pl.CostEstimate(flops=flops, bytes_accessed=moved, transcendentals=0),
    )(*args)


def iota(shape, axis):
    return lax.broadcasted_iota(I32, shape, axis)


def pack(sc, tok, cot, ids, wts, gate, up, down, out, w):
    wts_f = wts[...].astype(F32)
    named = jnp.zeros((EXP, TOK), F32)
    weight = jnp.zeros((EXP, TOK), F32)
    for k in range(8):
        match = iota((EXP, TOK), 0) == ids[k : k + 1, :]
        named += jnp.where(match, 1.0, 0.0)
        weight += jnp.where(match, wts_f[k : k + 1, :], 0.0)
    before = (iota((TOK, TOK), 0) < iota((TOK, TOK), 1)).astype(BF)
    rank = dot(named.astype(BF), before)
    code = jnp.concatenate([named * (rank + 1.0), weight], 0).astype(BF)
    spread = (iota((64, 128), 0) + 64 == iota((64, 128), 1)).astype(BF)
    meta = dot(code, spread, FIRST).astype(BF)
    low = iota((TOK, 128), 1) < 64
    out[:, 0:FEAT] = tok[...]
    out[:, 384:512] = jnp.where(low, out[:, 384:512], meta)
    out[:, 512 : 512 + FEAT] = cot[...]
    out[:, 896:1024] = jnp.where(low, out[:, 896:1024], jnp.zeros((TOK, 128), BF))
    w[0:FEAT, 0:512] = gate[...]
    w[0:FEAT, 512:1024] = up[...]
    w[0:FEAT, 1024:1536] = down[...]
    w[FEAT:WIDE, :] = jnp.zeros((WIDE - FEAT, 1536), BF)


def placed(code, block, core):
    place = code.astype(I32) - 1 + block * CAP + core * PART
    place = jnp.where(place >= ROWS, place - ROWS, place)
    return jnp.where(code > 0.5, place, -1)


def choose(sc, every, near, send):
    lanes = iota((8, 128), 1) - 64
    row = iota((8, 128), 0)
    sel = ((row == 0) & (lanes == sc[0])) | ((row == 1) & (lanes == sc[1]))
    codes = dot(sel.astype(BF), every[:, 384:512], LAST)
    block = (iota((1, ALL), 1) * 1639) >> 16
    for k, out in ((0, near), (1, send)):
        place = placed(codes[k : k + 1, :], block, sc[2])
        one_hot = (iota((ROWS, ALL), 0) == place).astype(BF)
        out[...] = dot(one_hot, every[...]).astype(BF)


def products(a, b, w, wf, lo):
    x = jnp.concatenate([a[lo : lo + PART, 0:512], b[lo : lo + PART, 0:512]], 0)
    dy = jnp.concatenate([a[lo : lo + PART, 512:1024], b[lo : lo + PART, 512:1024]], 0)
    for h, ref in ((0, w), (1, wf)):
        for c, left in ((0, x), (1, x), (2, dy)):
            yield 1536 * h + 512 * c, dot(left, ref[:, 512 * c : 512 * c + 512])


def forward_others(sc, near, far, w, wf, out):
    for at, value in products(near, far, w, wf, PART):
        out[:, at : at + 512] = value.astype(BF)


def forward_mine(sc, near, far, w, wf, got, out):
    for at, value in products(near, far, w, wf, 0):
        out[:, at : at + 512] = (value + got[:, at : at + 512].astype(F32)).astype(BF)


def activate(sc, pieces, near_tile, far_tile, g_out, s_out):
    q = ROWS // 4
    start = pl.multiple_of((sc[3] % 2) * q, 16)
    a = near_tile[pl.ds(start, q), :].astype(F32)
    b = far_tile[pl.ds(start, q), :].astype(F32)
    tile = jnp.where(sc[3] < 2, a, b)
    lane = iota((q, 128), 1)
    scale = jnp.sum(jnp.where(lane == 96 + sc[0], tile, 0.0), axis=1, keepdims=True)
    dots = jnp.zeros((q, 1), F32)
    for h in range(2):
        at = 1536 * h

        def total(c):
            cols = slice(at + 512 * c, at + 512 * c + 512)
            t = pieces[0, :, cols].astype(F32) + pieces[1, :, cols].astype(F32)
            return t + pieces[2, :, cols].astype(F32) + pieces[3, :, cols].astype(F32)

        gate_pre, up_pre, hidden_grad = total(0), total(1), total(2)
        sig = jax.nn.sigmoid(gate_pre)
        hidden = (gate_pre * sig * up_pre).astype(BF).astype(F32)
        dots += jnp.sum(hidden * hidden_grad, axis=1, keepdims=True)
        act_grad = scale * hidden_grad
        gate_g = (act_grad * up_pre * sig * (1.0 + gate_pre * (1.0 - sig))).astype(BF)
        up_g = (act_grad * gate_pre * sig).astype(BF)
        scaled = (scale * hidden).astype(BF)
        for k in range(4):
            g_out[k, :, 1024 * h : 1024 * h + 512] = gate_g
            g_out[k, :, 1024 * h + 512 : 1024 * h + 1024] = up_g
            s_out[k, :, 512 * h : 512 * h + 512] = scaled
    dot_tile = jnp.where(lane == 0, dots, 0.0).astype(BF)
    for k in range(4):
        g_out[k, :, 2048:2176] = dot_tile


def backward(sc, g, go, w, wf, keep, send):
    put = (iota((128, WIDE), 0) == 0) & (iota((128, WIDE), 1) == FEAT + sc[0])
    put = put.astype(BF)
    for lo, out in ((PART, send), (0, keep)):
        for at, ref in ((0, g), (PART, go)):
            t = dot(ref[lo : lo + PART, 0:1024], w[:, 0:1024], LAST)
            t += dot(ref[lo : lo + PART, 1024:2048], wf[:, 0:1024], LAST)
            t += dot(ref[lo : lo + PART, 2048:2176], put)
            out[at : at + PART, :] = t.astype(BF)


def weight_grads(sc, near, far, g, go, s, so, mine, partner):
    for c in range(3):
        at = 0 if c < 2 else 512
        total = [None, None]
        for rows, lo, right, right_s in (
            (near, 0, g, s),
            (far, 0, g, s),
            (near, PART, go, so),
            (far, PART, go, so),
        ):
            at_r = 0 if rows is near else PART
            left = rows[lo : lo + PART, at : at + 512]
            for h in range(2):
                r = right if c < 2 else right_s
                col = 1024 * h + 512 * c if c < 2 else 512 * h
                t = dot(left, r[at_r : at_r + PART, col : col + 512], FIRST)
                total[h] = t if total[h] is None else total[h] + t
        mine[:, 512 * c : 512 * c + 512] = total[0][:FEAT]
        partner[:, 512 * c : 512 * c + 512] = total[1][:FEAT].astype(BF)


def scatter(sc, tile, own, oth, *outs):
    lane = iota((ALL, 128), 1)
    block = (iota((ALL, 1), 0) * 1639) >> 16
    value = tile[...].astype(F32)
    total = None
    for k, slot in ((0, own), (1, oth)):
        code = jnp.sum(jnp.where(lane == 64 + sc[k], value, 0.0), axis=1, keepdims=True)
        place = placed(code, block, sc[2])
        if k == 0:
            hit = iota((ALL, ALL), 1) == place
        else:
            hit = hit | (iota((ALL, ALL), 1) == jnp.where(place >= 0, place + ROWS, -1))
    both = jnp.concatenate([own[...], oth[...]], 0)
    total = dot(hit.astype(BF), both)
    at = 0
    for out in outs:
        rows = out.shape[0]
        out[...] = total[at : at + rows].astype(BF)
        at += rows


def add_near(sc, far, a, b, c, d, e, first, mid, last):
    s = far[...].astype(F32) + a[...].astype(F32) + b[...].astype(F32)
    s = s + c[...].astype(F32) + d[...].astype(F32)
    first[...] = (s[:TOK] + e[...].astype(F32)).astype(BF)
    mid[...] = s[TOK : 2 * TOK]
    last[...] = s[2 * TOK :].astype(BF)


def finish_tokens(sc, mid, a, b, ids, tok, route):
    total = mid[...] + a[...].astype(F32) + b[...].astype(F32)
    tok[...] = total[:, :FEAT].astype(BF)
    sel = (iota((EXP, 128), 0) + 64 == iota((EXP, 128), 1)).astype(BF)
    dots = dot(sel, total[:, 384:512].astype(BF), LAST)
    for k in range(8):
        match = iota((EXP, TOK), 0) == ids[k : k + 1, :]
        route[k : k + 1, :] = jnp.sum(jnp.where(match, dots, 0.0), axis=0, keepdims=True)


def finish_weights(sc, mine, got, gate, up, down):
    for c, out in enumerate((gate, up, down)):
        cols = slice(512 * c, 512 * c + 512)
        out[...] = (mine[:, cols] + got[:, cols].astype(F32)).astype(BF)


def take(a, axis, step):
    n = lax.axis_size(axis)
    return lax.ppermute(a, axis, [((i + step) % n, i) for i in range(n)])


def swap_core(a):
    return lax.ppermute(a, "core", [(0, 1), (1, 0)])


def swap_half(a):
    return lax.ppermute(a, "y", [(0, 1), (1, 0), (2, 3), (3, 2)])


def swap_expert(a):
    return lax.ppermute(a, "y", [(1, 2), (2, 1), (3, 0), (0, 3)])


def trade(a, axis):
    return lax.all_to_all(a, axis, split_axis=0, concat_axis=0, tiled=True)


def on_device(tokens, cotangent, expert_ids, route_weight, gate_weight, up_weight, down_weight):
    core = lax.axis_index("core")
    high = (lax.axis_index("y") >= 2).astype(I32)
    z = lax.axis_index("z")
    sc = jnp.stack([2 * z + high, 2 * z + 1 - high, core, lax.axis_index("x")]).astype(I32)
    ids_t = expert_ids.T
    payload, w = call(
        pack,
        [((TOK, 1024), BF), ((WIDE, 1536), BF)],
        sc, tokens, cotangent, ids_t, route_weight.T,
        gate_weight[0], up_weight[0], down_weight[0].T,
    )
    five = take(payload, "z", 5)
    minus = take(payload, "z", -5)
    group = jnp.concatenate([five, payload, minus], 0)
    near_z = [take(group, "z", step) for step in (1, -1, 2, -2)]
    eight = take(five, "z", 3)
    w_far = swap_half(w)
    every = jnp.concatenate([group] + near_z + [eight], 0)
    every, w_far = lax.optimization_barrier((every, w_far))
    near, send = call(
        choose, [((ROWS, 1024), BF)] * 2, sc, every, flops=4 * ROWS * ALL * 1024
    )
    far = swap_expert(send)
    flops = 2 * ROWS * WIDE * 3072
    others = call(
        forward_others, [((ROWS, 3072), BF)], sc, near, far, w, w_far, flops=flops
    )[0]
    pair = call(
        forward_mine, [((ROWS, 3072), BF)], sc, near, far, w, w_far, swap_core(others), flops=flops
    )[0]
    q = ROWS // 4
    pieces = trade(pair.reshape(4, q, 3072), "x")
    g_out, s_out = call(
        activate, [((4, q, 2176), BF), ((4, q, 1024), BF)],
        sc, pieces, near[:PART, 384:512], far[:PART, 384:512],
    )
    g = trade(g_out, "x")
    s_out, g = lax.optimization_barrier((s_out, g))
    s = trade(s_out, "x").reshape(ROWS, 1024)
    g = g.reshape(ROWS, 2176)
    g_far = swap_core(g)
    keep, away = call(backward, [((ROWS, WIDE), BF)] * 2, sc, g, g_far, w, w_far)
    back = swap_expert(away)
    s_far = swap_core(s)
    mine_w, partner_w = call(
        weight_grads, [((FEAT, 1536), F32), ((FEAT, 1536), BF)],
        sc, near, far, g, g_far, s, s_far, flops=8 * ROWS * WIDE * 1536,
    )
    got_w = swap_half(partner_w)
    sums = call(
        scatter, [((3 * TOK, WIDE), BF)] * 5 + [((TOK, WIDE), BF)],
        sc, every[:, 384:512], keep, back, flops=2 * ALL * ALL * WIDE,
    )
    moved = [take(a, "z", -step) for a, step in zip(sums[1:5], (1, -1, 2, -2))]
    moved.append(take(sums[5], "z", -3))
    first, mid, last = call(
        add_near, [((TOK, WIDE), BF), ((TOK, WIDE), F32), ((TOK, WIDE), BF)], sc, sums[0], *moved
    )
    from_first, from_last = take(first, "z", -5), take(last, "z", 5)
    from_first, from_last, got_w = lax.optimization_barrier((from_first, from_last, got_w))
    tok, route = call(
        finish_tokens, [((TOK, FEAT), BF), ((8, TOK), F32)], sc, mid, from_first, from_last, ids_t
    )
    gate, up, down = call(finish_weights, [((FEAT, 512), BF)] * 3, sc, mine_w, got_w)
    return (tok, route.astype(BF).T, gate[None], up[None], down.T[None])


def solution(mesh):
    fine = Mesh(mesh.devices.reshape(4, 2, 16, 4), ("x", "core", "z", "y"))
    dp, expert = ("x", "core"), ("z", "y")
    return jax.shard_map(
        on_device,
        mesh=fine,
        in_specs=(
            P(expert, dp),
            P(expert, dp),
            P(expert, None),
            P(expert, None),
            P(expert, dp, None),
            P(expert, dp, None),
            P(expert, None, dp),
        ),
        out_specs=(
            P(expert, dp),
            P(expert, None),
            P(expert, dp, None),
            P(expert, dp, None),
            P(expert, None, dp),
        ),
        check_vma=False,
    )
```

```python
import jax
import jax.numpy as jnp
from jax import lax
from jax.experimental import pallas as pl
from jax.experimental.pallas import tpu as pltpu
from jax.sharding import Mesh, PartitionSpec as P

BF = jnp.bfloat16
F32 = jnp.float32
I32 = jnp.int32
TOK = 40
FEAT = 448
WIDE = 512
HALF = 512
CAP = 20
ALL = 640
PART = 160
ROWS = 320
EXP = 32


def dot(a, b, dims=((1,), (0,))):
    return lax.dot_general(a, b, (dims, ((), ())), preferred_element_type=F32)


LAST = ((1,), (1,))
FIRST = ((0,), (0,))


def call(body, outs, *args, flops=0, own_copies=False):
    moved = sum(a.size * a.dtype.itemsize for a in args[1:])

    def whole(shape):
        if own_copies:
            return pl.BlockSpec(shape, lambda i: (0,) * len(shape))
        return pl.BlockSpec(memory_space=pltpu.VMEM)

    return pl.pallas_call(
        body,
        grid=(1,) if own_copies else (),
        out_shape=[jax.ShapeDtypeStruct(s, d) for s, d in outs],
        in_specs=[pl.BlockSpec(memory_space=pltpu.SMEM)] + [whole(a.shape) for a in args[1:]],
        out_specs=[whole(shape) for shape, _ in outs],
        compiler_params=pltpu.CompilerParams(vmem_limit_bytes=(52 if own_copies else 24) << 20),
        cost_estimate=pl.CostEstimate(flops=flops, bytes_accessed=moved, transcendentals=0),
    )(*args)


def iota(shape, axis):
    return lax.broadcasted_iota(I32, shape, axis)


def pack(sc, tok, cot, ids, wts, out):
    wts_f = wts[...].astype(F32)
    named = jnp.zeros((EXP, TOK), F32)
    weight = jnp.zeros((EXP, TOK), F32)
    for k in range(8):
        match = iota((EXP, TOK), 0) == ids[k : k + 1, :]
        named += jnp.where(match, 1.0, 0.0)
        weight += jnp.where(match, wts_f[k : k + 1, :], 0.0)
    before = (iota((TOK, TOK), 0) < iota((TOK, TOK), 1)).astype(BF)
    rank = dot(named.astype(BF), before)
    code = jnp.concatenate([named * (rank + 1.0), weight], 0).astype(BF)
    spread = (iota((64, 128), 0) + 64 == iota((64, 128), 1)).astype(BF)
    meta = dot(code, spread, FIRST).astype(BF)
    low = iota((TOK, 128), 1) < 64
    out[:, 0:FEAT] = tok[...]
    out[:, 384:512] = jnp.where(low, out[:, 384:512], meta)
    out[:, 512 : 512 + FEAT] = cot[...]
    out[:, 896:1024] = jnp.where(low, out[:, 896:1024], jnp.zeros((TOK, 128), BF))


def pack_weights(sc, gate, up, down, w):
    w[0:FEAT, 0:512] = gate[...]
    w[0:FEAT, 512:1024] = up[...]
    w[0:FEAT, 1024:1536] = down[...]
    w[FEAT:WIDE, :] = jnp.zeros((WIDE - FEAT, 1536), BF)


def placed(code, block, core):
    place = code.astype(I32) - 1 + block * CAP + core * PART
    place = jnp.where(place >= ROWS, place - ROWS, place)
    return jnp.where(code > 0.5, place, -1)


def choose(sc, every, near, send):
    lanes = iota((8, 128), 1) - 64
    row = iota((8, 128), 0)
    sel = ((row == 0) & (lanes == sc[0])) | ((row == 1) & (lanes == sc[1]))
    codes = dot(sel.astype(BF), every[:, 384:512], LAST)
    block = (iota((1, ALL), 1) * 1639) >> 16
    for k, out in ((0, near), (1, send)):
        place = placed(codes[k : k + 1, :], block, sc[2])
        one_hot = (iota((ROWS, ALL), 0) == place).astype(BF)
        out[...] = dot(one_hot, every[...]).astype(BF)


def products(rows, w, wf, lo):
    x, dy = rows[lo : lo + PART, 0:512], rows[lo : lo + PART, 512:1024]
    for h, ref in ((0, w), (1, wf)):
        for c, left in ((0, x), (1, x), (2, dy)):
            yield 1536 * h + 512 * c, dot(left, ref[:, 512 * c : 512 * c + 512])


def forward_others(sc, rows, w, wf, out):
    for at, value in products(rows, w, wf, PART):
        out[:, at : at + 512] = value.astype(BF)


def forward_mine(sc, near, far, w, wf, got_near, got_far, out):
    for lo, rows, got in ((0, near, got_near), (PART, far, got_far)):
        for at, value in products(rows, w, wf, 0):
            total = value + got[:, at : at + 512].astype(F32)
            out[lo : lo + PART, at : at + 512] = total.astype(BF)


def activate(sc, pieces, near_tile, far_tile, g_out):
    q = ROWS // 4
    start = pl.multiple_of((sc[3] % 2) * q, 16)
    a = near_tile[pl.ds(start, q), :].astype(F32)
    b = far_tile[pl.ds(start, q), :].astype(F32)
    tile = jnp.where(sc[3] < 2, a, b)
    lane = iota((q, 128), 1)
    scale = jnp.sum(jnp.where(lane == 96 + sc[0], tile, 0.0), axis=1, keepdims=True)
    dots = jnp.zeros((q, 1), F32)
    for h in range(2):
        at = 1536 * h

        def total(c):
            cols = slice(at + 512 * c, at + 512 * c + 512)
            t = pieces[0, :, cols].astype(F32) + pieces[1, :, cols].astype(F32)
            return t + pieces[2, :, cols].astype(F32) + pieces[3, :, cols].astype(F32)

        gate_pre, up_pre, hidden_grad = total(0), total(1), total(2)
        sig = jax.nn.sigmoid(gate_pre)
        hidden = (gate_pre * sig * up_pre).astype(BF).astype(F32)
        dots += jnp.sum(hidden * hidden_grad, axis=1, keepdims=True)
        act_grad = scale * hidden_grad
        gate_g = (act_grad * up_pre * sig * (1.0 + gate_pre * (1.0 - sig))).astype(BF)
        up_g = (act_grad * gate_pre * sig).astype(BF)
        scaled = (scale * hidden).astype(BF)
        for k in range(4):
            g_out[k, :, 1024 * h : 1024 * h + 512] = gate_g
            g_out[k, :, 1024 * h + 512 : 1024 * h + 1024] = up_g
            g_out[k, :, 2176 + 512 * h : 2688 + 512 * h] = scaled
    dot_tile = jnp.where(lane == 0, dots, 0.0).astype(BF)
    for k in range(4):
        g_out[k, :, 2048:2176] = dot_tile


def backward(lo):
    def body(sc, g, go, w, wf, out):
        put = (iota((128, WIDE), 0) == 0) & (iota((128, WIDE), 1) == FEAT + sc[0])
        put = put.astype(BF)
        for at, ref in ((0, g), (PART, go)):
            t = dot(ref[lo : lo + PART, 0:1024], w[:, 0:1024], LAST)
            t += dot(ref[lo : lo + PART, 1024:2048], wf[:, 0:1024], LAST)
            t += dot(ref[lo : lo + PART, 2048:2176], put)
            out[at : at + PART, :] = t.astype(BF)

    return body


def weight_grads(sc, near, far, g, go, mine, partner):
    for c in range(3):
        at = 0 if c < 2 else 512
        for h in range(2):
            col = 1024 * h + 512 * c if c < 2 else 2176 + 512 * h
            cols = slice(col, col + 512)
            t = dot(near[0:PART, at : at + 512], g[0:PART, cols], FIRST)
            t += dot(far[0:PART, at : at + 512], g[PART:ROWS, cols], FIRST)
            t += dot(near[PART:ROWS, at : at + 512], go[0:PART, cols], FIRST)
            t += dot(far[PART:ROWS, at : at + 512], go[PART:ROWS, cols], FIRST)
            out = slice(512 * c, 512 * c + 512)
            if h == 0:
                mine[:, out] = t[:FEAT]
            else:
                partner[:, out] = t[:FEAT].astype(BF)


def scatter(sc, tile, own, oth, *outs):
    lane = iota((ALL, 128), 1)
    block = (iota((ALL, 1), 0) * 1639) >> 16
    value = tile[...].astype(F32)
    total = None
    for k, slot in ((0, own), (1, oth)):
        code = jnp.sum(jnp.where(lane == 64 + sc[k], value, 0.0), axis=1, keepdims=True)
        place = placed(code, block, sc[2])
        if k == 0:
            hit = iota((ALL, ALL), 1) == place
        else:
            hit = hit | (iota((ALL, ALL), 1) == jnp.where(place >= 0, place + ROWS, -1))
    both = jnp.concatenate([own[...], oth[...]], 0)
    total = dot(hit.astype(BF), both)
    at = 0
    for out in outs:
        rows = out.shape[0]
        out[...] = total[at : at + rows].astype(BF)
        at += rows


def add_near(sc, far, a, b, c, d, e, first, mid, last):
    s = far[...].astype(F32) + a[...].astype(F32) + b[...].astype(F32)
    s = s + c[...].astype(F32) + d[...].astype(F32)
    first[...] = (s[:TOK] + e[...].astype(F32)).astype(BF)
    mid[...] = s[TOK : 2 * TOK]
    last[...] = s[2 * TOK :].astype(BF)


def finish_tokens(sc, mid, a, b, ids, tok, route):
    total = mid[...] + a[...].astype(F32) + b[...].astype(F32)
    tok[...] = total[:, :FEAT].astype(BF)
    sel = (iota((EXP, 128), 0) + 64 == iota((EXP, 128), 1)).astype(BF)
    dots = dot(sel, total[:, 384:512].astype(BF), LAST)
    out = jnp.zeros((8, TOK), F32)
    for k in range(8):
        match = iota((EXP, TOK), 0) == ids[k : k + 1, :]
        row = jnp.sum(jnp.where(match, dots, 0.0), axis=0, keepdims=True)
        out += jnp.where(iota((8, TOK), 0) == k, row, 0.0)
    route[...] = out.astype(BF)


def finish_weights(sc, mine, got, gate, up, down):
    for c, out in enumerate((gate, up, down)):
        cols = slice(512 * c, 512 * c + 512)
        out[...] = (mine[:, cols] + got[:, cols].astype(F32)).astype(BF)


def take(a, axis, step):
    n = lax.axis_size(axis)
    return lax.ppermute(a, axis, [((i + step) % n, i) for i in range(n)])


def swap_core(a):
    return lax.ppermute(a, "core", [(0, 1), (1, 0)])


def swap_half(a):
    return lax.ppermute(a, "y", [(0, 1), (1, 0), (2, 3), (3, 2)])


def swap_expert(a):
    return lax.ppermute(a, "y", [(1, 2), (2, 1), (3, 0), (0, 3)])


def trade(a, axis):
    return lax.all_to_all(a, axis, split_axis=0, concat_axis=0, tiled=True)


def on_device(tokens, cotangent, expert_ids, route_weight, gate_weight, up_weight, down_weight):
    core = lax.axis_index("core")
    high = (lax.axis_index("y") >= 2).astype(I32)
    z = lax.axis_index("z")
    sc = jnp.stack([2 * z + high, 2 * z + 1 - high, core, lax.axis_index("x")]).astype(I32)
    ids_t = expert_ids.T
    (payload,) = call(
        pack, [((TOK, 1024), BF)], sc, tokens, cotangent, ids_t, route_weight.T, own_copies=True
    )
    payload, gate_m, up_m, down_m = lax.optimization_barrier(
        (payload, gate_weight[0], up_weight[0], down_weight[0].T)
    )
    (w,) = call(pack_weights, [((WIDE, 1536), BF)], sc, gate_m, up_m, down_m, own_copies=True)
    five = take(payload, "z", 5)
    minus = take(payload, "z", -5)
    group = jnp.concatenate([five, payload, minus], 0)
    near_z = [take(group, "z", step) for step in (1, -1, 2, -2)]
    eight = take(five, "z", 3)
    w_far = swap_half(w)
    every = jnp.concatenate([group] + near_z + [eight], 0)
    near, send = call(
        choose, [((ROWS, 1024), BF)] * 2, sc, every, flops=0
    )
    far = swap_expert(send)
    flops = 2 * PART * WIDE * 3072
    out = [((PART, 3072), BF)]
    (near_others,) = call(forward_others, out, sc, near, w, w_far, flops=flops)
    (far_others,) = call(forward_others, out, sc, far, w, w_far, flops=flops)
    (pair,) = call(
        forward_mine, [((ROWS, 3072), BF)],
        sc, near, far, w, w_far, swap_core(near_others), swap_core(far_others), flops=2 * flops,
    )
    q = ROWS // 4
    pieces = trade(pair.reshape(4, q, 3072), "x")
    (g_out,) = call(
        activate, [((4, q, 3200), BF)], sc, pieces, near[:PART, 384:512], far[:PART, 384:512]
    )
    g = trade(g_out, "x").reshape(ROWS, 3200)
    g_far = swap_core(g)
    (away,) = call(backward(PART), [((ROWS, WIDE), BF)], sc, g, g_far, w, w_far)
    back = swap_expert(away)
    near_w, far_w, g, _ = lax.optimization_barrier((near, far, g, away))
    (keep,) = call(backward(0), [((ROWS, WIDE), BF)], sc, g, g_far, w, w_far)
    mine_w, partner_w = call(
        weight_grads, [((FEAT, 1536), F32), ((FEAT, 1536), BF)],
        sc, near_w, far_w, g, g_far, flops=8 * ROWS * WIDE * 1536,
    )
    got_w = swap_half(partner_w)
    sums = call(
        scatter, [((3 * TOK, WIDE), BF)] * 5 + [((TOK, WIDE), BF)],
        sc, every[:, 384:512], keep, back, flops=30 * 10**9,
    )
    moved = [take(a, "z", -step) for a, step in zip(sums[1:5], (1, -1, 2, -2))]
    moved.append(take(sums[5], "z", -3))
    first, mid, last = call(
        add_near, [((TOK, WIDE), BF), ((TOK, WIDE), F32), ((TOK, WIDE), BF)], sc, sums[0], *moved
    )
    got_w, mid = lax.optimization_barrier((got_w, mid))
    gate, up, down = call(finish_weights, [((FEAT, 512), BF)] * 3, sc, mine_w, got_w)
    from_first, from_last = take(first, "z", -5), take(last, "z", 5)
    from_first, from_last, gate, up, down = lax.optimization_barrier(
        (from_first, from_last, gate, up, down)
    )
    tok, route = call(
        finish_tokens, [((TOK, FEAT), BF), ((8, TOK), BF)], sc, mid, from_first, from_last, ids_t
    )
    return (tok, route.T, gate[None], up[None], down.T[None])


def solution(mesh):
    fine = Mesh(mesh.devices.reshape(4, 2, 16, 4), ("x", "core", "z", "y"))
    dp, expert = ("x", "core"), ("z", "y")
    return jax.shard_map(
        on_device,
        mesh=fine,
        in_specs=(
            P(expert, dp),
            P(expert, dp),
            P(expert, None),
            P(expert, None),
            P(expert, dp, None),
            P(expert, dp, None),
            P(expert, None, dp),
        ),
        out_specs=(
            P(expert, dp),
            P(expert, None),
            P(expert, dp, None),
            P(expert, dp, None),
            P(expert, None, dp),
        ),
        check_vma=False,
    )
```

```python
import jax
import jax.numpy as jnp
from jax import lax
from jax.experimental import pallas as pl
from jax.experimental.pallas import tpu as pltpu
from jax.sharding import Mesh, PartitionSpec as P

BF = jnp.bfloat16
F32 = jnp.float32
I32 = jnp.int32
TOK = 40
FEAT = 448
WIDE = 512
HALF = 512
CAP = 20
ALL = 640
PART = 160
ROWS = 320
EXP = 32


def dot(a, b, dims=((1,), (0,))):
    return lax.dot_general(a, b, (dims, ((), ())), preferred_element_type=F32)


LAST = ((1,), (1,))
FIRST = ((0,), (0,))


def call(body, outs, *args, flops=0, own_copies=False):
    moved = sum(a.size * a.dtype.itemsize for a in args[1:])

    def whole(shape):
        if own_copies:
            return pl.BlockSpec(shape, lambda i: (0,) * len(shape))
        return pl.BlockSpec(memory_space=pltpu.VMEM)

    return pl.pallas_call(
        body,
        grid=(1,) if own_copies else (),
        out_shape=[jax.ShapeDtypeStruct(s, d) for s, d in outs],
        in_specs=[pl.BlockSpec(memory_space=pltpu.SMEM)] + [whole(a.shape) for a in args[1:]],
        out_specs=[whole(shape) for shape, _ in outs],
        compiler_params=pltpu.CompilerParams(vmem_limit_bytes=(52 if own_copies else 24) << 20),
        cost_estimate=pl.CostEstimate(flops=flops, bytes_accessed=moved, transcendentals=0),
    )(*args)


def iota(shape, axis):
    return lax.broadcasted_iota(I32, shape, axis)


def pack(sc, both, slots, out):
    named = jnp.zeros((EXP, TOK), F32)
    weight = jnp.zeros((EXP, TOK), F32)
    for k in range(8):
        match = iota((EXP, TOK), 0).astype(F32) == slots[k : k + 1, :]
        named += jnp.where(match, 1.0, 0.0)
        weight += jnp.where(match, slots[8 + k : 9 + k, :], 0.0)
    before = (iota((TOK, TOK), 0) < iota((TOK, TOK), 1)).astype(BF)
    rank = dot(named.astype(BF), before)
    code = jnp.concatenate([named * (rank + 1.0), weight], 0).astype(BF)
    spread = (iota((64, 128), 0) + 64 == iota((64, 128), 1)).astype(BF)
    meta = dot(code, spread, FIRST).astype(BF)
    low = iota((TOK, 128), 1) < 64
    out[:, 0:FEAT] = both[:, 0:FEAT]
    out[:, 384:512] = jnp.where(low, out[:, 384:512], meta)
    out[:, 512 : 512 + FEAT] = both[:, 512 : 512 + FEAT]
    out[:, 896:1024] = jnp.where(low, out[:, 896:1024], jnp.zeros((TOK, 128), BF))


def pack_weights(sc, gate, up, down, w):
    w[0:FEAT, 0:512] = gate[...]
    w[0:FEAT, 512:1024] = up[...]
    w[0:FEAT, 1024:1536] = down[...]
    w[FEAT:WIDE, :] = jnp.zeros((WIDE - FEAT, 1536), BF)


def placed(code, block, core):
    place = code.astype(I32) - 1 + block * CAP + core * PART
    place = jnp.where(place >= ROWS, place - ROWS, place)
    return jnp.where(code > 0.5, place, -1)


def choose(sc, every, near, send):
    lanes = iota((8, 128), 1) - 64
    row = iota((8, 128), 0)
    sel = ((row == 0) & (lanes == sc[0])) | ((row == 1) & (lanes == sc[1]))
    codes = dot(sel.astype(BF), every[:, 384:512], LAST)
    block = (iota((1, ALL), 1) * 1639) >> 16
    for k, out in ((0, near), (1, send)):
        place = placed(codes[k : k + 1, :], block, sc[2])
        one_hot = (iota((ROWS, ALL), 0) == place).astype(BF)
        out[...] = dot(one_hot, every[...]).astype(BF)


def products(rows, w, wf, lo):
    x, dy = rows[lo : lo + PART, 0:512], rows[lo : lo + PART, 512:1024]
    for h, ref in ((0, w), (1, wf)):
        for c, left in ((0, x), (1, x), (2, dy)):
            yield 1536 * h + 512 * c, dot(left, ref[:, 512 * c : 512 * c + 512])


def forward_others(sc, rows, w, wf, out):
    for at, value in products(rows, w, wf, PART):
        out[:, at : at + 512] = value.astype(BF)


def forward_mine(sc, near, far, w, wf, got_near, got_far, out):
    for lo, rows, got in ((0, near, got_near), (PART, far, got_far)):
        for at, value in products(rows, w, wf, 0):
            total = value + got[:, at : at + 512].astype(F32)
            out[lo : lo + PART, at : at + 512] = total.astype(BF)


def activate(sc, pieces, near_tile, far_tile, g_out):
    q = ROWS // 4
    start = pl.multiple_of((sc[3] % 2) * q, 16)
    a = near_tile[pl.ds(start, q), :].astype(F32)
    b = far_tile[pl.ds(start, q), :].astype(F32)
    tile = jnp.where(sc[3] < 2, a, b)
    lane = iota((q, 128), 1)
    scale = jnp.sum(jnp.where(lane == 96 + sc[0], tile, 0.0), axis=1, keepdims=True)
    dots = jnp.zeros((q, 1), F32)
    for h in range(2):
        at = 1536 * h

        def total(c):
            cols = slice(at + 512 * c, at + 512 * c + 512)
            t = pieces[0, :, cols].astype(F32) + pieces[1, :, cols].astype(F32)
            return t + pieces[2, :, cols].astype(F32) + pieces[3, :, cols].astype(F32)

        gate_pre, up_pre, hidden_grad = total(0), total(1), total(2)
        sig = jax.nn.sigmoid(gate_pre)
        hidden = (gate_pre * sig * up_pre).astype(BF).astype(F32)
        dots += jnp.sum(hidden * hidden_grad, axis=1, keepdims=True)
        act_grad = scale * hidden_grad
        gate_g = (act_grad * up_pre * sig * (1.0 + gate_pre * (1.0 - sig))).astype(BF)
        up_g = (act_grad * gate_pre * sig).astype(BF)
        scaled = (scale * hidden).astype(BF)
        for k in range(4):
            g_out[k, :, 1024 * h : 1024 * h + 512] = gate_g
            g_out[k, :, 1024 * h + 512 : 1024 * h + 1024] = up_g
            g_out[k, :, 2176 + 512 * h : 2688 + 512 * h] = scaled
    dot_tile = jnp.where(lane == 0, dots, 0.0).astype(BF)
    for k in range(4):
        g_out[k, :, 2048:2176] = dot_tile


def back_rows(sc, g, lo, rows, w, wf):
    put = (iota((128, WIDE), 0) == 0) & (iota((128, WIDE), 1) == FEAT + sc[0])
    t = dot(g[lo : lo + rows, 0:1024], w[:, 0:1024], LAST)
    t += dot(g[lo : lo + rows, 1024:2048], wf[:, 0:1024], LAST)
    t += dot(g[lo : lo + rows, 2048:2176], put.astype(BF))
    return t.astype(BF)


def backward_mine(sc, g, w, wf, out):
    out[...] = back_rows(sc, g, 0, ROWS, w, wf)


def backward_others(lo):
    def body(sc, go, w, wf, mine, out):
        out[0:PART, :] = mine[lo : lo + PART, :]
        out[PART:ROWS, :] = back_rows(sc, go, lo, PART, w, wf)

    return body


def weight_grads(sc, near, far, g, go, mine, partner):
    for c in range(3):
        at = 0 if c < 2 else 512
        for h in range(2):
            col = 1024 * h + 512 * c if c < 2 else 2176 + 512 * h
            cols = slice(col, col + 512)
            t = dot(near[0:PART, at : at + 512], g[0:PART, cols], FIRST)
            t += dot(far[0:PART, at : at + 512], g[PART:ROWS, cols], FIRST)
            t += dot(near[PART:ROWS, at : at + 512], go[0:PART, cols], FIRST)
            t += dot(far[PART:ROWS, at : at + 512], go[PART:ROWS, cols], FIRST)
            out = slice(512 * c, 512 * c + 512)
            if h == 0:
                mine[:, out] = t[:FEAT]
            else:
                partner[:, out] = t[:FEAT].astype(BF)


def scatter(sc, tile, own, oth, *outs):
    lane = iota((ALL, 128), 1)
    block = (iota((ALL, 1), 0) * 1639) >> 16
    value = tile[...].astype(F32)
    total = None
    for k, slot in ((0, own), (1, oth)):
        code = jnp.sum(jnp.where(lane == 64 + sc[k], value, 0.0), axis=1, keepdims=True)
        place = placed(code, block, sc[2])
        if k == 0:
            hit = iota((ALL, ALL), 1) == place
        else:
            hit = hit | (iota((ALL, ALL), 1) == jnp.where(place >= 0, place + ROWS, -1))
    both = jnp.concatenate([own[...], oth[...]], 0)
    total = dot(hit.astype(BF), both)
    at = 0
    for out in outs:
        rows = out.shape[0]
        out[...] = total[at : at + rows].astype(BF)
        at += rows


def add_near(sc, far, a, b, c, d, e, first, mid, last):
    s = far[...].astype(F32) + a[...].astype(F32) + b[...].astype(F32)
    s = s + c[...].astype(F32) + d[...].astype(F32)
    first[...] = (s[:TOK] + e[...].astype(F32)).astype(BF)
    mid[...] = s[TOK : 2 * TOK]
    last[...] = s[2 * TOK :].astype(BF)


def finish_tokens(sc, mid, a, b, ids, tok, route):
    total = mid[...] + a[...].astype(F32) + b[...].astype(F32)
    tok[...] = total[:, :FEAT].astype(BF)
    sel = (iota((EXP, 128), 0) + 64 == iota((EXP, 128), 1)).astype(BF)
    dots = dot(sel, total[:, 384:512].astype(BF), LAST)
    out = jnp.zeros((8, TOK), F32)
    for k in range(8):
        match = iota((EXP, TOK), 0) == ids[k : k + 1, :]
        row = jnp.sum(jnp.where(match, dots, 0.0), axis=0, keepdims=True)
        out += jnp.where(iota((8, TOK), 0) == k, row, 0.0)
    route[...] = out.astype(BF)


def finish_weights(sc, mine, got, gate, up, down):
    for c, out in enumerate((gate, up, down)):
        cols = slice(512 * c, 512 * c + 512)
        out[...] = (mine[:, cols] + got[:, cols].astype(F32)).astype(BF)


def take(a, axis, step):
    n = lax.axis_size(axis)
    return lax.ppermute(a, axis, [((i + step) % n, i) for i in range(n)])


def swap_core(a):
    return lax.ppermute(a, "core", [(0, 1), (1, 0)])


def swap_half(a):
    return lax.ppermute(a, "y", [(0, 1), (1, 0), (2, 3), (3, 2)])


def swap_expert(a):
    return lax.ppermute(a, "y", [(1, 2), (2, 1), (3, 0), (0, 3)])


def trade(a, axis):
    return lax.all_to_all(a, axis, split_axis=0, concat_axis=0, tiled=True)


def on_device(tokens, cotangent, expert_ids, route_weight, gate_weight, up_weight, down_weight):
    core = lax.axis_index("core")
    high = (lax.axis_index("y") >= 2).astype(I32)
    z = lax.axis_index("z")
    sc = jnp.stack([2 * z + high, 2 * z + 1 - high, core, lax.axis_index("x")]).astype(I32)
    ids_t = expert_ids.T
    both = jnp.concatenate([tokens, jnp.zeros((TOK, 64), BF), cotangent], 1)
    slots = jnp.concatenate([ids_t.astype(F32), route_weight.T.astype(F32)], 0)
    (payload,) = call(pack, [((TOK, 1024), BF)], sc, both, slots)
    payload, gate_m, up_m, down_m = lax.optimization_barrier(
        (payload, gate_weight[0], up_weight[0], down_weight[0].T)
    )
    (w,) = call(pack_weights, [((WIDE, 1536), BF)], sc, gate_m, up_m, down_m, own_copies=True)
    five = take(payload, "z", 5)
    minus = take(payload, "z", -5)
    group = jnp.concatenate([five, payload, minus], 0)
    near_z = [take(group, "z", step) for step in (1, -1, 2, -2)]
    eight = take(five, "z", 3)
    w_far = swap_half(w)
    every = jnp.concatenate([group] + near_z + [eight], 0)
    near, send = call(
        choose, [((ROWS, 1024), BF)] * 2, sc, every, flops=0
    )
    far = swap_expert(send)
    flops = 2 * PART * WIDE * 3072
    out = [((PART, 3072), BF)]
    (near_others,) = call(forward_others, out, sc, near, w, w_far, flops=flops)
    (far_others,) = call(forward_others, out, sc, far, w, w_far, flops=flops)
    (pair,) = call(
        forward_mine, [((ROWS, 3072), BF)],
        sc, near, far, w, w_far, swap_core(near_others), swap_core(far_others), flops=2 * flops,
    )
    q = ROWS // 4
    pieces = trade(pair.reshape(4, q, 3072), "x")
    (g_out,) = call(
        activate, [((4, q, 3200), BF)], sc, pieces, near[:PART, 384:512], far[:PART, 384:512]
    )
    g = trade(g_out, "x").reshape(ROWS, 3200)
    g_far = swap_core(g)
    (back_mine,) = call(backward_mine, [((ROWS, WIDE), BF)], sc, g, w, w_far)
    out = [((ROWS, WIDE), BF)]
    (away,) = call(backward_others(PART), out, sc, g_far, w, w_far, back_mine)
    back = swap_expert(away)
    near_w, far_w, g, _ = lax.optimization_barrier((near, far, g, away))
    (keep,) = call(backward_others(0), out, sc, g_far, w, w_far, back_mine)
    mine_w, partner_w = call(
        weight_grads, [((FEAT, 1536), F32), ((FEAT, 1536), BF)],
        sc, near_w, far_w, g, g_far, flops=8 * ROWS * WIDE * 1536,
    )
    got_w = swap_half(partner_w)
    sums = call(
        scatter, [((3 * TOK, WIDE), BF)] * 5 + [((TOK, WIDE), BF)],
        sc, every[:, 384:512], keep, back, flops=30 * 10**9,
    )
    order = ((1, 1), (3, 2), (2, -1), (4, -2), (5, 3))
    moved = [take(sums[slot], "z", -step) for slot, step in order]
    first, mid, last = call(
        add_near, [((TOK, WIDE), BF), ((TOK, WIDE), F32), ((TOK, WIDE), BF)], sc, sums[0], *moved
    )
    got_w, mid = lax.optimization_barrier((got_w, mid))
    gate, up, down = call(finish_weights, [((FEAT, 512), BF)] * 3, sc, mine_w, got_w)
    from_first, from_last = take(first, "z", -5), take(last, "z", 5)
    from_first, from_last, gate, up, down = lax.optimization_barrier(
        (from_first, from_last, gate, up, down)
    )
    tok, route = call(
        finish_tokens, [((TOK, FEAT), BF), ((8, TOK), BF)], sc, mid, from_first, from_last, ids_t
    )
    return (tok, route.T, gate[None], up[None], down.T[None])


def solution(mesh):
    fine = Mesh(mesh.devices.reshape(4, 2, 16, 4), ("x", "core", "z", "y"))
    dp, expert = ("x", "core"), ("z", "y")
    return jax.shard_map(
        on_device,
        mesh=fine,
        in_specs=(
            P(expert, dp),
            P(expert, dp),
            P(expert, None),
            P(expert, None),
            P(expert, dp, None),
            P(expert, dp, None),
            P(expert, None, dp),
        ),
        out_specs=(
            P(expert, dp),
            P(expert, None),
            P(expert, dp, None),
            P(expert, dp, None),
            P(expert, None, dp),
        ),
        check_vma=False,
    )
```

```python
import jax
import jax.numpy as jnp
from jax import lax
from jax.experimental import pallas as pl
from jax.experimental.pallas import tpu as pltpu
from jax.sharding import Mesh, PartitionSpec as P

BF = jnp.bfloat16
F32 = jnp.float32
I32 = jnp.int32
TOK = 40
FEAT = 448
WIDE = 512
HALF = 512
CAP = 20
ALL = 640
PART = 160
ROWS = 320
EXP = 32


def dot(a, b, dims=((1,), (0,))):
    return lax.dot_general(a, b, (dims, ((), ())), preferred_element_type=F32)


LAST = ((1,), (1,))
FIRST = ((0,), (0,))


def call(body, outs, *args, flops=0, own_copies=False):
    moved = sum(a.size * a.dtype.itemsize for a in args[1:])

    def whole(shape):
        if own_copies:
            return pl.BlockSpec(shape, lambda i: (0,) * len(shape))
        return pl.BlockSpec(memory_space=pltpu.VMEM)

    return pl.pallas_call(
        body,
        grid=(1,) if own_copies else (),
        out_shape=[jax.ShapeDtypeStruct(s, d) for s, d in outs],
        in_specs=[pl.BlockSpec(memory_space=pltpu.SMEM)] + [whole(a.shape) for a in args[1:]],
        out_specs=[whole(shape) for shape, _ in outs],
        compiler_params=pltpu.CompilerParams(vmem_limit_bytes=(52 if own_copies else 24) << 20),
        cost_estimate=pl.CostEstimate(flops=flops, bytes_accessed=moved, transcendentals=0),
    )(*args)


def iota(shape, axis):
    return lax.broadcasted_iota(I32, shape, axis)


def pack(sc, both, slots, out):
    named = jnp.zeros((EXP, TOK), F32)
    weight = jnp.zeros((EXP, TOK), F32)
    for k in range(8):
        match = iota((EXP, TOK), 0).astype(F32) == slots[k : k + 1, :]
        named += jnp.where(match, 1.0, 0.0)
        weight += jnp.where(match, slots[8 + k : 9 + k, :], 0.0)
    before = (iota((TOK, TOK), 0) < iota((TOK, TOK), 1)).astype(BF)
    rank = dot(named.astype(BF), before)
    code = jnp.concatenate([named * (rank + 1.0), weight], 0).astype(BF)
    spread = (iota((64, 128), 0) + 64 == iota((64, 128), 1)).astype(BF)
    meta = dot(code, spread, FIRST).astype(BF)
    low = iota((TOK, 128), 1) < 64
    out[:, 0:FEAT] = both[:, 0:FEAT]
    out[:, 384:512] = jnp.where(low, out[:, 384:512], meta)
    out[:, 512 : 512 + FEAT] = both[:, 512 : 512 + FEAT]
    out[:, 896:1024] = jnp.where(low, out[:, 896:1024], jnp.zeros((TOK, 128), BF))


def pack_weights(sc, gate, up, down, w):
    w[0:FEAT, 0:512] = gate[...]
    w[0:FEAT, 512:1024] = up[...]
    w[0:FEAT, 1024:1536] = down[...]
    w[FEAT:WIDE, :] = jnp.zeros((WIDE - FEAT, 1536), BF)


def placed(code, block, core):
    place = code.astype(I32) - 1 + block * CAP + core * PART
    place = jnp.where(place >= ROWS, place - ROWS, place)
    return jnp.where(code > 0.5, place, -1)


def choose(sc, every, near, send):
    lanes = iota((8, 128), 1) - 64
    row = iota((8, 128), 0)
    sel = ((row == 0) & (lanes == sc[0])) | ((row == 1) & (lanes == sc[1]))
    codes = dot(sel.astype(BF), every[:, 384:512], LAST)
    block = (iota((1, ALL), 1) * 1639) >> 16
    for k, out in ((0, near), (1, send)):
        place = placed(codes[k : k + 1, :], block, sc[2])
        one_hot = (iota((ROWS, ALL), 0) == place).astype(BF)
        out[...] = dot(one_hot, every[...]).astype(BF)


def products(rows, w, wf, lo):
    x, dy = rows[lo : lo + PART, 0:512], rows[lo : lo + PART, 512:1024]
    for h, ref in ((0, w), (1, wf)):
        for c, left in ((0, x), (1, x), (2, dy)):
            yield 1536 * h + 512 * c, dot(left, ref[:, 512 * c : 512 * c + 512])


def forward_others(sc, rows, w, wf, out):
    for at, value in products(rows, w, wf, PART):
        out[:, at : at + 512] = value.astype(BF)


def forward_mine(sc, near, far, w, wf, got_near, got_far, out):
    for lo, rows, got in ((0, near, got_near), (PART, far, got_far)):
        for at, value in products(rows, w, wf, 0):
            total = value + got[:, at : at + 512].astype(F32)
            out[lo : lo + PART, at : at + 512] = total.astype(BF)


def activate(sc, pieces, near_tile, far_tile, g_out):
    q = ROWS // 4
    start = pl.multiple_of((sc[3] % 2) * q, 16)
    a = near_tile[pl.ds(start, q), 384:512].astype(F32)
    b = far_tile[pl.ds(start, q), 384:512].astype(F32)
    tile = jnp.where(sc[3] < 2, a, b)
    lane = iota((q, 128), 1)
    scale = jnp.sum(jnp.where(lane == 96 + sc[0], tile, 0.0), axis=1, keepdims=True)
    dots = jnp.zeros((q, 1), F32)
    for h in range(2):
        at = 1536 * h

        def total(c):
            cols = slice(at + 512 * c, at + 512 * c + 512)
            t = pieces[0, :, cols].astype(F32) + pieces[1, :, cols].astype(F32)
            return t + pieces[2, :, cols].astype(F32) + pieces[3, :, cols].astype(F32)

        gate_pre, up_pre, hidden_grad = total(0), total(1), total(2)
        sig = jax.nn.sigmoid(gate_pre)
        hidden = (gate_pre * sig * up_pre).astype(BF).astype(F32)
        dots += jnp.sum(hidden * hidden_grad, axis=1, keepdims=True)
        act_grad = scale * hidden_grad
        gate_g = (act_grad * up_pre * sig * (1.0 + gate_pre * (1.0 - sig))).astype(BF)
        up_g = (act_grad * gate_pre * sig).astype(BF)
        scaled = (scale * hidden).astype(BF)
        for k in range(4):
            g_out[k, :, 1024 * h : 1024 * h + 512] = gate_g
            g_out[k, :, 1024 * h + 512 : 1024 * h + 1024] = up_g
            g_out[k, :, 2176 + 512 * h : 2688 + 512 * h] = scaled
    dot_tile = jnp.where(lane == 0, dots, 0.0).astype(BF)
    for k in range(4):
        g_out[k, :, 2048:2176] = dot_tile


def back_rows(sc, g, lo, rows, w, wf):
    put = (iota((128, WIDE), 0) == 0) & (iota((128, WIDE), 1) == FEAT + sc[0])
    t = dot(g[lo : lo + rows, 0:1024], w[:, 0:1024], LAST)
    t += dot(g[lo : lo + rows, 1024:2048], wf[:, 0:1024], LAST)
    t += dot(g[lo : lo + rows, 2048:2176], put.astype(BF))
    return t.astype(BF)


def backward_mine(sc, g, w, wf, out):
    out[...] = back_rows(sc, g, 0, ROWS, w, wf)


def backward_others(lo):
    def body(sc, go, w, wf, mine, out):
        out[0:PART, :] = mine[lo : lo + PART, :]
        out[PART:ROWS, :] = back_rows(sc, go, lo, PART, w, wf)

    return body


def weight_grads(sc, near, far, g, go, mine, partner):
    for c in range(3):
        at = 0 if c < 2 else 512
        for h in range(2):
            col = 1024 * h + 512 * c if c < 2 else 2176 + 512 * h
            cols = slice(col, col + 512)
            t = dot(near[0:PART, at : at + 512], g[0:PART, cols], FIRST)
            t += dot(far[0:PART, at : at + 512], g[PART:ROWS, cols], FIRST)
            t += dot(near[PART:ROWS, at : at + 512], go[0:PART, cols], FIRST)
            t += dot(far[PART:ROWS, at : at + 512], go[PART:ROWS, cols], FIRST)
            out = slice(512 * c, 512 * c + 512)
            if h == 0:
                mine[:, out] = t[:FEAT]
            else:
                partner[:, out] = t[:FEAT].astype(BF)


def scatter(sc, tile, own, oth, *outs):
    lane = iota((ALL, 128), 1)
    block = (iota((ALL, 1), 0) * 1639) >> 16
    value = tile[...].astype(F32)
    total = None
    for k, slot in ((0, own), (1, oth)):
        code = jnp.sum(jnp.where(lane == 64 + sc[k], value, 0.0), axis=1, keepdims=True)
        place = placed(code, block, sc[2])
        if k == 0:
            hit = iota((ALL, ALL), 1) == place
        else:
            hit = hit | (iota((ALL, ALL), 1) == jnp.where(place >= 0, place + ROWS, -1))
    both = jnp.concatenate([own[...], oth[...]], 0)
    total = dot(hit.astype(BF), both)
    at = 0
    for out in outs:
        rows = out.shape[0]
        out[...] = total[at : at + rows].astype(BF)
        at += rows


def add_near(sc, far, a, b, c, d, e, first, mid, last):
    s = far[...].astype(F32) + a[...].astype(F32) + b[...].astype(F32)
    s = s + c[...].astype(F32) + d[...].astype(F32)
    first[...] = (s[:TOK] + e[...].astype(F32)).astype(BF)
    mid[...] = s[TOK : 2 * TOK]
    last[...] = s[2 * TOK :].astype(BF)


def finish_tokens(sc, mid, a, b, ids, tok, route):
    total = mid[...] + a[...].astype(F32) + b[...].astype(F32)
    tok[...] = total[:, :FEAT].astype(BF)
    sel = (iota((EXP, 128), 0) + 64 == iota((EXP, 128), 1)).astype(BF)
    dots = dot(sel, total[:, 384:512].astype(BF), LAST)
    out = jnp.zeros((8, TOK), F32)
    for k in range(8):
        match = iota((EXP, TOK), 0) == ids[k : k + 1, :]
        row = jnp.sum(jnp.where(match, dots, 0.0), axis=0, keepdims=True)
        out += jnp.where(iota((8, TOK), 0) == k, row, 0.0)
    route[...] = out.astype(BF)


def finish_weights(sc, mine, got, gate, up, down):
    for c, out in enumerate((gate, up, down)):
        cols = slice(512 * c, 512 * c + 512)
        out[...] = (mine[:, cols] + got[:, cols].astype(F32)).astype(BF)


def take(a, axis, step):
    n = lax.axis_size(axis)
    return lax.ppermute(a, axis, [((i + step) % n, i) for i in range(n)])


def swap_core(a):
    return lax.ppermute(a, "core", [(0, 1), (1, 0)])


def swap_half(a):
    return lax.ppermute(a, "y", [(0, 1), (1, 0), (2, 3), (3, 2)])


def swap_expert(a):
    return lax.ppermute(a, "y", [(1, 2), (2, 1), (3, 0), (0, 3)])


def trade(a, axis):
    return lax.all_to_all(a, axis, split_axis=0, concat_axis=0, tiled=True)


def on_device(tokens, cotangent, expert_ids, route_weight, gate_weight, up_weight, down_weight):
    core = lax.axis_index("core")
    high = (lax.axis_index("y") >= 2).astype(I32)
    z = lax.axis_index("z")
    sc = jnp.stack([2 * z + high, 2 * z + 1 - high, core, lax.axis_index("x")]).astype(I32)
    ids_t = expert_ids.T
    both = jnp.concatenate([tokens, jnp.zeros((TOK, 64), BF), cotangent], 1)
    slots = jnp.concatenate([ids_t.astype(F32), route_weight.T.astype(F32)], 0)
    (payload,) = call(pack, [((TOK, 1024), BF)], sc, both, slots)
    payload, gate_m, up_m, down_m = lax.optimization_barrier(
        (payload, gate_weight[0], up_weight[0], down_weight[0].T)
    )
    (w,) = call(pack_weights, [((WIDE, 1536), BF)], sc, gate_m, up_m, down_m, own_copies=True)
    five = take(payload, "z", 5)
    minus = take(payload, "z", -5)
    group = jnp.concatenate([five, payload, minus], 0)
    near_z = [take(group, "z", step) for step in (1, -1, 2, -2)]
    eight = take(five, "z", 3)
    w_far = swap_half(w)
    every = jnp.concatenate([group] + near_z + [eight], 0)
    near, send = call(
        choose, [((ROWS, 1024), BF)] * 2, sc, every, flops=0
    )
    far = swap_expert(send)
    flops = 2 * PART * WIDE * 3072
    out = [((PART, 3072), BF)]
    (near_others,) = call(forward_others, out, sc, near, w, w_far, flops=flops)
    (far_others,) = call(forward_others, out, sc, far, w, w_far, flops=flops)
    (pair,) = call(
        forward_mine, [((ROWS, 3072), BF)],
        sc, near, far, w, w_far, swap_core(near_others), swap_core(far_others), flops=2 * flops,
    )
    q = ROWS // 4
    pieces = trade(pair.reshape(4, q, 3072), "x")
    (g_out,) = call(
        activate, [((4, q, 3200), BF)], sc, pieces, near, far
    )
    g = trade(g_out, "x").reshape(ROWS, 3200)
    g_far = swap_core(g)
    (back_mine,) = call(backward_mine, [((ROWS, WIDE), BF)], sc, g, w, w_far)
    out = [((ROWS, WIDE), BF)]
    (away,) = call(backward_others(PART), out, sc, g_far, w, w_far, back_mine)
    back = swap_expert(away)
    near_w, far_w, g, _ = lax.optimization_barrier((near, far, g, away))
    (keep,) = call(backward_others(0), out, sc, g_far, w, w_far, back_mine)
    mine_w, partner_w = call(
        weight_grads, [((FEAT, 1536), F32), ((FEAT, 1536), BF)],
        sc, near_w, far_w, g, g_far, flops=8 * ROWS * WIDE * 1536,
    )
    got_w = swap_half(partner_w)
    sums = call(
        scatter, [((3 * TOK, WIDE), BF)] * 5 + [((TOK, WIDE), BF)],
        sc, every[:, 384:512], keep, back, flops=30 * 10**9,
    )
    order = ((1, 1), (3, 2), (2, -1), (4, -2), (5, 3))
    moved = [take(sums[slot], "z", -step) for slot, step in order]
    first, mid, last = call(
        add_near, [((TOK, WIDE), BF), ((TOK, WIDE), F32), ((TOK, WIDE), BF)], sc, sums[0], *moved
    )
    got_w, mid = lax.optimization_barrier((got_w, mid))
    gate, up, down = call(finish_weights, [((FEAT, 512), BF)] * 3, sc, mine_w, got_w)
    from_first, from_last = take(first, "z", -5), take(last, "z", 5)
    from_first, from_last, gate, up, down = lax.optimization_barrier(
        (from_first, from_last, gate, up, down)
    )
    tok, route = call(
        finish_tokens, [((TOK, FEAT), BF), ((8, TOK), BF)], sc, mid, from_first, from_last, ids_t
    )
    return (tok, route.T, gate[None], up[None], down.T[None])


def solution(mesh):
    fine = Mesh(mesh.devices.reshape(4, 2, 16, 4), ("x", "core", "z", "y"))
    dp, expert = ("x", "core"), ("z", "y")
    return jax.shard_map(
        on_device,
        mesh=fine,
        in_specs=(
            P(expert, dp),
            P(expert, dp),
            P(expert, None),
            P(expert, None),
            P(expert, dp, None),
            P(expert, dp, None),
            P(expert, None, dp),
        ),
        out_specs=(
            P(expert, dp),
            P(expert, None),
            P(expert, dp, None),
            P(expert, dp, None),
            P(expert, None, dp),
        ),
        check_vma=False,
    )
```

```python
import jax
import jax.numpy as jnp
from jax import lax
from jax.experimental import pallas as pl
from jax.experimental.pallas import tpu as pltpu
from jax.sharding import Mesh, PartitionSpec as P

BF = jnp.bfloat16
F32 = jnp.float32
I32 = jnp.int32
TOK = 40
FEAT = 448
WIDE = 512
HALF = 512
CAP = 20
ALL = 640
PART = 160
ROWS = 320
EXP = 32


def dot(a, b, dims=((1,), (0,))):
    return lax.dot_general(a, b, (dims, ((), ())), preferred_element_type=F32)


LAST = ((1,), (1,))
FIRST = ((0,), (0,))


def call(body, outs, *args, flops=0, own_copies=False):
    moved = sum(a.size * a.dtype.itemsize for a in args[1:])

    def whole(shape):
        if own_copies:
            return pl.BlockSpec(shape, lambda i: (0,) * len(shape))
        return pl.BlockSpec(memory_space=pltpu.VMEM)

    return pl.pallas_call(
        body,
        grid=(1,) if own_copies else (),
        out_shape=[jax.ShapeDtypeStruct(s, d) for s, d in outs],
        in_specs=[pl.BlockSpec(memory_space=pltpu.SMEM)] + [whole(a.shape) for a in args[1:]],
        out_specs=[whole(shape) for shape, _ in outs],
        compiler_params=pltpu.CompilerParams(vmem_limit_bytes=(52 if own_copies else 24) << 20),
        cost_estimate=pl.CostEstimate(flops=flops, bytes_accessed=moved, transcendentals=0),
    )(*args)


def iota(shape, axis):
    return lax.broadcasted_iota(I32, shape, axis)


def pack(sc, both, slots, out):
    named = jnp.zeros((EXP, TOK), F32)
    weight = jnp.zeros((EXP, TOK), F32)
    for k in range(8):
        match = iota((EXP, TOK), 0).astype(F32) == slots[k : k + 1, :]
        named += jnp.where(match, 1.0, 0.0)
        weight += jnp.where(match, slots[8 + k : 9 + k, :], 0.0)
    before = (iota((TOK, TOK), 0) < iota((TOK, TOK), 1)).astype(BF)
    rank = dot(named.astype(BF), before)
    code = jnp.concatenate([named * (rank + 1.0), weight], 0).astype(BF)
    spread = (iota((64, 128), 0) + 64 == iota((64, 128), 1)).astype(BF)
    meta = dot(code, spread, FIRST).astype(BF)
    low = iota((TOK, 128), 1) < 64
    out[:, 0:FEAT] = both[:, 0:FEAT]
    out[:, 384:512] = jnp.where(low, out[:, 384:512], meta)
    out[:, 512 : 512 + FEAT] = both[:, 512 : 512 + FEAT]
    out[:, 896:1024] = jnp.where(low, out[:, 896:1024], jnp.zeros((TOK, 128), BF))


def pack_weights(sc, gate, up, down, w):
    w[0:FEAT, 0:512] = gate[...]
    w[0:FEAT, 512:1024] = up[...]
    w[0:FEAT, 1024:1536] = down[...]
    w[FEAT:WIDE, :] = jnp.zeros((WIDE - FEAT, 1536), BF)


def placed(code, block, core):
    place = code.astype(I32) - 1 + block * CAP + core * PART
    place = jnp.where(place >= ROWS, place - ROWS, place)
    return jnp.where(code > 0.5, place, -1)


def choose(k):
    def body(sc, every, out):
        lanes = iota((8, 128), 1) - 64
        codes = dot((lanes == sc[k]).astype(BF), every[:, 384:512], LAST)
        block = (iota((1, ALL), 1) * 1639) >> 16
        place = placed(codes[0:1, :], block, sc[2])
        one_hot = (iota((ROWS, ALL), 0) == place).astype(BF)
        out[...] = dot(one_hot, every[...]).astype(BF)

    return body


def products(rows, w, wf, lo):
    x, dy = rows[lo : lo + PART, 0:512], rows[lo : lo + PART, 512:1024]
    for h, ref in ((0, w), (1, wf)):
        for c, left in ((0, x), (1, x), (2, dy)):
            yield 1536 * h + 512 * c, dot(left, ref[:, 512 * c : 512 * c + 512])


def forward_others(sc, rows, w, wf, out):
    for at, value in products(rows, w, wf, PART):
        out[:, at : at + 512] = value.astype(BF)


def forward_mine(sc, near, far, w, wf, got_near, got_far, out):
    for lo, rows, got in ((0, near, got_near), (PART, far, got_far)):
        for at, value in products(rows, w, wf, 0):
            total = value + got[:, at : at + 512].astype(F32)
            out[lo : lo + PART, at : at + 512] = total.astype(BF)


def activate(sc, pieces, near_tile, far_tile, g_out):
    q = ROWS // 4
    start = pl.multiple_of((sc[3] % 2) * q, 16)
    a = near_tile[pl.ds(start, q), 384:512].astype(F32)
    b = far_tile[pl.ds(start, q), 384:512].astype(F32)
    tile = jnp.where(sc[3] < 2, a, b)
    lane = iota((q, 128), 1)
    scale = jnp.sum(jnp.where(lane == 96 + sc[0], tile, 0.0), axis=1, keepdims=True)
    dots = jnp.zeros((q, 1), F32)
    for h in range(2):
        at = 1536 * h

        def total(c):
            cols = slice(at + 512 * c, at + 512 * c + 512)
            t = pieces[0, :, cols].astype(F32) + pieces[1, :, cols].astype(F32)
            return t + pieces[2, :, cols].astype(F32) + pieces[3, :, cols].astype(F32)

        gate_pre, up_pre, hidden_grad = total(0), total(1), total(2)
        sig = jax.nn.sigmoid(gate_pre)
        hidden = (gate_pre * sig * up_pre).astype(BF).astype(F32)
        dots += jnp.sum(hidden * hidden_grad, axis=1, keepdims=True)
        act_grad = scale * hidden_grad
        gate_g = (act_grad * up_pre * sig * (1.0 + gate_pre * (1.0 - sig))).astype(BF)
        up_g = (act_grad * gate_pre * sig).astype(BF)
        scaled = (scale * hidden).astype(BF)
        for k in range(4):
            g_out[k, :, 1024 * h : 1024 * h + 512] = gate_g
            g_out[k, :, 1024 * h + 512 : 1024 * h + 1024] = up_g
            g_out[k, :, 2176 + 512 * h : 2688 + 512 * h] = scaled
    dot_tile = jnp.where(lane == 0, dots, 0.0).astype(BF)
    for k in range(4):
        g_out[k, :, 2048:2176] = dot_tile


def back_rows(sc, g, lo, rows, w, wf):
    put = (iota((128, WIDE), 0) == 0) & (iota((128, WIDE), 1) == FEAT + sc[0])
    t = dot(g[lo : lo + rows, 0:1024], w[:, 0:1024], LAST)
    t += dot(g[lo : lo + rows, 1024:2048], wf[:, 0:1024], LAST)
    t += dot(g[lo : lo + rows, 2048:2176], put.astype(BF))
    return t.astype(BF)


def backward_mine(sc, g, w, wf, out):
    out[...] = back_rows(sc, g, 0, ROWS, w, wf)


def backward_others(lo):
    def body(sc, go, w, wf, mine, out):
        out[0:PART, :] = mine[lo : lo + PART, :]
        out[PART:ROWS, :] = back_rows(sc, go, lo, PART, w, wf)

    return body


def weight_grads(sc, near, far, g, go, mine, partner):
    for c in range(3):
        at = 0 if c < 2 else 512
        for h in range(2):
            col = 1024 * h + 512 * c if c < 2 else 2176 + 512 * h
            cols = slice(col, col + 512)
            t = dot(near[0:PART, at : at + 512], g[0:PART, cols], FIRST)
            t += dot(far[0:PART, at : at + 512], g[PART:ROWS, cols], FIRST)
            t += dot(near[PART:ROWS, at : at + 512], go[0:PART, cols], FIRST)
            t += dot(far[PART:ROWS, at : at + 512], go[PART:ROWS, cols], FIRST)
            out = slice(512 * c, 512 * c + 512)
            if h == 0:
                mine[:, out] = t[:FEAT]
            else:
                partner[:, out] = t[:FEAT].astype(BF)


def scatter(sc, tile, own, oth, *outs):
    lane = iota((ALL, 128), 1)
    block = (iota((ALL, 1), 0) * 1639) >> 16
    value = tile[...].astype(F32)
    total = None
    for k, slot in ((0, own), (1, oth)):
        code = jnp.sum(jnp.where(lane == 64 + sc[k], value, 0.0), axis=1, keepdims=True)
        place = placed(code, block, sc[2])
        if k == 0:
            hit = iota((ALL, ALL), 1) == place
        else:
            hit = hit | (iota((ALL, ALL), 1) == jnp.where(place >= 0, place + ROWS, -1))
    both = jnp.concatenate([own[...], oth[...]], 0)
    total = dot(hit.astype(BF), both)
    at = 0
    for out in outs:
        rows = out.shape[0]
        out[...] = total[at : at + rows].astype(BF)
        at += rows


def add_near(sc, far, a, b, c, d, e, first, mid, last):
    s = far[...].astype(F32) + a[...].astype(F32) + b[...].astype(F32)
    s = s + c[...].astype(F32) + d[...].astype(F32)
    first[...] = (s[:TOK] + e[...].astype(F32)).astype(BF)
    mid[...] = s[TOK : 2 * TOK]
    last[...] = s[2 * TOK :].astype(BF)


def finish_tokens(sc, mid, a, b, ids, tok, route):
    total = mid[...] + a[...].astype(F32) + b[...].astype(F32)
    tok[...] = total[:, :FEAT].astype(BF)
    sel = (iota((EXP, 128), 0) + 64 == iota((EXP, 128), 1)).astype(BF)
    dots = dot(sel, total[:, 384:512].astype(BF), LAST)
    out = jnp.zeros((8, TOK), F32)
    for k in range(8):
        match = iota((EXP, TOK), 0) == ids[k : k + 1, :]
        row = jnp.sum(jnp.where(match, dots, 0.0), axis=0, keepdims=True)
        out += jnp.where(iota((8, TOK), 0) == k, row, 0.0)
    route[...] = out.astype(BF)


def finish_weights(sc, mine, got, gate, up, down):
    for c, out in enumerate((gate, up, down)):
        cols = slice(512 * c, 512 * c + 512)
        out[...] = (mine[:, cols] + got[:, cols].astype(F32)).astype(BF)


def take(a, axis, step):
    n = lax.axis_size(axis)
    return lax.ppermute(a, axis, [((i + step) % n, i) for i in range(n)])


def swap_core(a):
    return lax.ppermute(a, "core", [(0, 1), (1, 0)])


def swap_half(a):
    return lax.ppermute(a, "y", [(0, 1), (1, 0), (2, 3), (3, 2)])


def swap_expert(a):
    return lax.ppermute(a, "y", [(1, 2), (2, 1), (3, 0), (0, 3)])


def trade(a, axis):
    return lax.all_to_all(a, axis, split_axis=0, concat_axis=0, tiled=True)


def on_device(tokens, cotangent, expert_ids, route_weight, gate_weight, up_weight, down_weight):
    core = lax.axis_index("core")
    high = (lax.axis_index("y") >= 2).astype(I32)
    z = lax.axis_index("z")
    sc = jnp.stack([2 * z + high, 2 * z + 1 - high, core, lax.axis_index("x")]).astype(I32)
    ids_t = expert_ids.T
    both = jnp.concatenate([tokens, jnp.zeros((TOK, 64), BF), cotangent], 1)
    slots = jnp.concatenate([ids_t.astype(F32), route_weight.T.astype(F32)], 0)
    (payload,) = call(pack, [((TOK, 1024), BF)], sc, both, slots)
    payload, gate_m, up_m, down_m = lax.optimization_barrier(
        (payload, gate_weight[0], up_weight[0], down_weight[0].T)
    )
    (w,) = call(pack_weights, [((WIDE, 1536), BF)], sc, gate_m, up_m, down_m, own_copies=True)
    five = take(payload, "z", 5)
    minus = take(payload, "z", -5)
    group = jnp.concatenate([five, payload, minus], 0)
    near_z = [take(group, "z", step) for step in (1, -1, 2, -2)]
    eight = take(five, "z", 3)
    w_far = swap_half(w)
    every = jnp.concatenate([group] + near_z + [eight], 0)
    picked = [((ROWS, 1024), BF)]
    (send,) = call(choose(1), picked, sc, every)
    later, send = lax.optimization_barrier((every, send))
    (near,) = call(choose(0), picked, sc, later)
    far = swap_expert(send)
    flops = 2 * PART * WIDE * 3072
    out = [((PART, 3072), BF)]
    (near_others,) = call(forward_others, out, sc, near, w, w_far, flops=flops)
    (far_others,) = call(forward_others, out, sc, far, w, w_far, flops=flops)
    (pair,) = call(
        forward_mine, [((ROWS, 3072), BF)],
        sc, near, far, w, w_far, swap_core(near_others), swap_core(far_others), flops=2 * flops,
    )
    q = ROWS // 4
    pieces = trade(pair.reshape(4, q, 3072), "x")
    (g_out,) = call(
        activate, [((4, q, 3200), BF)], sc, pieces, near, far
    )
    g = trade(g_out, "x").reshape(ROWS, 3200)
    g_far = swap_core(g)
    (back_mine,) = call(backward_mine, [((ROWS, WIDE), BF)], sc, g, w, w_far)
    out = [((ROWS, WIDE), BF)]
    (away,) = call(backward_others(PART), out, sc, g_far, w, w_far, back_mine)
    back = swap_expert(away)
    near_w, far_w, g, _ = lax.optimization_barrier((near, far, g, away))
    (keep,) = call(backward_others(0), out, sc, g_far, w, w_far, back_mine)
    mine_w, partner_w = call(
        weight_grads, [((FEAT, 1536), F32), ((FEAT, 1536), BF)],
        sc, near_w, far_w, g, g_far, flops=8 * ROWS * WIDE * 1536,
    )
    got_w = swap_half(partner_w)
    sums = call(
        scatter, [((3 * TOK, WIDE), BF)] * 5 + [((TOK, WIDE), BF)],
        sc, every[:, 384:512], keep, back, flops=30 * 10**9,
    )
    order = ((1, 1), (3, 2), (2, -1), (4, -2), (5, 3))
    moved = [take(sums[slot], "z", -step) for slot, step in order]
    first, mid, last = call(
        add_near, [((TOK, WIDE), BF), ((TOK, WIDE), F32), ((TOK, WIDE), BF)], sc, sums[0], *moved
    )
    got_w, mid = lax.optimization_barrier((got_w, mid))
    gate, up, down = call(finish_weights, [((FEAT, 512), BF)] * 3, sc, mine_w, got_w)
    from_first, from_last = take(first, "z", -5), take(last, "z", 5)
    from_first, from_last, gate, up, down = lax.optimization_barrier(
        (from_first, from_last, gate, up, down)
    )
    tok, route = call(
        finish_tokens, [((TOK, FEAT), BF), ((8, TOK), BF)], sc, mid, from_first, from_last, ids_t
    )
    return (tok, route.T, gate[None], up[None], down.T[None])


def solution(mesh):
    fine = Mesh(mesh.devices.reshape(4, 2, 16, 4), ("x", "core", "z", "y"))
    dp, expert = ("x", "core"), ("z", "y")
    return jax.shard_map(
        on_device,
        mesh=fine,
        in_specs=(
            P(expert, dp),
            P(expert, dp),
            P(expert, None),
            P(expert, None),
            P(expert, dp, None),
            P(expert, dp, None),
            P(expert, None, dp),
        ),
        out_specs=(
            P(expert, dp),
            P(expert, None),
            P(expert, dp, None),
            P(expert, dp, None),
            P(expert, None, dp),
        ),
        check_vma=False,
    )
```
